512 devices in a mesh: dp: 32 (over z, x), ctx: 16 (over y, core).
Axes of the slice: x: 4, y: 8, z: 8, core: 2. Of those that a mesh axis runs over, the one named last changes fastest.
Arguments:
- query: bfloat16 [64, 1024, 4096], P('dp', 'ctx'), may hold values from -6 to 6
- key_in: bfloat16 [64, 1024, 1024], P('dp', 'ctx'), may hold values from -6 to 6
- value_in: bfloat16 [64, 1024, 1024], P('dp', 'ctx'), may hold values from -6 to 6
- out_grad: bfloat16 [64, 1024, 4096], P('dp', 'ctx'), may hold values from -1.5 to 1.5
- masked: int32 [64, 512], P('dp'), may hold values from 0 to 1023, as said below
- bucket: int32 [64, 1024], P('dp', 'ctx'), may hold values from 0 to 15
Outputs:
- query_grad: bfloat16 [64, 1024, 4096], P('dp', 'ctx')
- key_grad: bfloat16 [64, 1024, 1024], P('dp', 'ctx')
- value_grad: bfloat16 [64, 1024, 1024], P('dp', 'ctx')
- bias_query_grad: float32 [16, 256], P('ctx', 'dp')
- bias_kv_grad: float32 [2, 1024], P(None, 'dp')
The draws below stay inside these ranges and needn't reach their ends.
Inputs may be any that keep to these rules, and one draw needn't show every extreme that they name: Each document has exactly 512 distinct masked positions.
All inputs are finite; a program needn't handle non-finite values.
Results may differ from the reference program's by a relative error of at most 0.012.
The reference program's roundings to bfloat16 on the way count: a program that leaves them out, or rounds other values in their place, can miss the bound.
Values may be sent and summed in bfloat16 or wider, within the bound.
A program may use at most 64 MiB of HBM per device.

```python
import math
import jax
import jax.numpy as jnp
from jax import lax

H = 32
KVH = 8
HD = 128
NB = 16
L = 1024
DOCS = 64
MASKED = 512
N_CTX = 16


def draw_query(key, part):
    normal_part = jnp.clip(jax.random.normal(jax.random.fold_in(key, 1), (DOCS, L, H * HD), jnp.float32), -6.0, 6.0)
    return normal_part.astype(jnp.bfloat16)


def draw_key_in(key, part):
    normal_part = jnp.clip(jax.random.normal(jax.random.fold_in(key, 3), (DOCS, L, KVH * HD), jnp.float32), -6.0, 6.0)
    return normal_part.astype(jnp.bfloat16)


def draw_masked(key, part):
    doc_keys = jax.random.split(jax.random.fold_in(key, 7), DOCS)
    orders = jax.vmap(lambda one_key: jax.random.permutation(one_key, L))(doc_keys)
    return orders[:, :MASKED].astype(jnp.int32)


def with_ends(result, own_key, least, top_value):
    shape = result.shape
    place = [jax.random.randint(jax.random.fold_in(own_key, axis), (), 0, shape[axis]) for axis in range(len(shape))]
    result = result.at[tuple(place)].set(least)
    longest = shape.index(max(shape))
    place[longest] = (place[longest] + 1) % shape[longest]
    return result.at[tuple(place)].set(top_value)


def shard_levels(own_key, shape, pieces, least, high):
    loudness = 1.0
    for position, parts in pieces:
        draws = jax.random.uniform(jax.random.fold_in(jax.random.fold_in(own_key, 6), position), (parts,), jnp.float32, least / len(pieces), high / len(pieces))
        loudness = loudness * jnp.repeat(jnp.exp(draws), shape[position] // parts).reshape((-1,) + (1,) * (len(shape) - 1 - position))
    return loudness


def centred(own_key, dims, scale, reach, cuts=(), held_as=jnp.bfloat16):
    drawn = scale * jax.random.normal(own_key, dims, jnp.float32)
    if cuts:
        drawn = drawn * shard_levels(own_key, dims, cuts, -0.22, 0.18)
    return jnp.clip(drawn, -reach, reach).astype(held_as)


def setup_inputs(seed: int = 0) -> dict:
    splits = jax.random.split(jax.random.key(seed), 7)
    return {
        "query": draw_query(jax.random.fold_in(splits[6], 71), 0),
        "key_in": draw_key_in(jax.random.fold_in(splits[6], 71), 0),
        "value_in": centred(splits[2], (DOCS, L, KVH * HD), 1.0, 6.0, ((0, 32), (1, 16))),
        "out_grad": centred(splits[3], (DOCS, L, H * HD), 0.25, 1.5, ((0, 32), (1, 16))),
        "masked": draw_masked(jax.random.fold_in(splits[6], 71), 0),
        "bucket": with_ends(jax.random.randint(splits[5], (DOCS, L), 0, NB), jax.random.fold_in(splits[5], 1), 0, NB - 1).astype(jnp.int32),
    }


def softmax_rows(scores):
    shifted = scores - lax.optimization_barrier(jnp.max(scores, axis=-1, keepdims=True))
    exponent = jnp.exp(shifted)
    return exponent / lax.optimization_barrier(jnp.sum(exponent, axis=-1, keepdims=True))

def head_group(inputs):
    queries, key_one, value_one, cot_group = inputs
    inv_root = 1.0 / math.sqrt(HD)
    query_float = queries.astype(jnp.float32)
    key_float = key_one.astype(jnp.float32)
    value_float = value_one.astype(jnp.float32)
    cot_float = cot_group.astype(jnp.float32)
    scores = jnp.einsum('hqd,kd->hqk', query_float, key_float) * inv_root
    attn_probs = softmax_rows(scores)
    probs_float = lax.optimization_barrier(attn_probs.astype(jnp.bfloat16)).astype(jnp.float32)
    attn_out = jnp.einsum('hqk,kd->hqd', probs_float, value_float)
    delta_rows = lax.optimization_barrier(jnp.sum(cot_float * attn_out, axis=-1))
    value_full = jnp.einsum('hqk,hqd->kd', probs_float, cot_float)
    prob_grad = jnp.einsum('hqd,kd->hqk', cot_float, value_float)
    score_low = (attn_probs * (prob_grad - delta_rows[..., None]) * inv_root).astype(jnp.bfloat16)
    score_float = lax.optimization_barrier(score_low).astype(jnp.float32)
    query_full = jnp.einsum('hqk,kd->hqd', score_float, key_float)
    key_full = jnp.einsum('hqk,hqd->kd', score_float, query_float)
    return (query_full, key_full, value_full)

def one_document(inputs):
    query_doc, key_doc, value_doc, cot_doc = inputs
    group_size = H // KVH
    query_groups = query_doc.reshape(L, KVH, group_size, HD).transpose(1, 2, 0, 3)
    cot_groups = cot_doc.reshape(L, KVH, group_size, HD).transpose(1, 2, 0, 3)
    key_heads = key_doc.reshape(L, KVH, HD).transpose(1, 0, 2)
    value_heads = value_doc.reshape(L, KVH, HD).transpose(1, 0, 2)
    query_full, key_full, value_full = lax.map(head_group, (query_groups, key_heads, value_heads, cot_groups))
    query_rows = query_full.transpose(2, 0, 1, 3).reshape(L, H * HD)
    key_rows = key_full.transpose(1, 0, 2).reshape(L, KVH * HD)
    value_rows = value_full.transpose(1, 0, 2).reshape(L, KVH * HD)
    return (query_rows.astype(jnp.bfloat16), lax.optimization_barrier(jnp.sum(query_rows, axis=0)), key_rows.astype(jnp.bfloat16), lax.optimization_barrier(jnp.sum(key_rows, axis=0)), value_rows.astype(jnp.bfloat16), lax.optimization_barrier(jnp.sum(value_rows, axis=0)))

def reference(query, key_in, value_in, out_grad, masked, bucket):
    positions = jnp.arange(L, dtype=jnp.int32)
    is_masked = jnp.any(masked[:, :, None] == positions[None, None, :], axis=1)
    loss_weight = is_masked.astype(jnp.float32) * NB / (bucket.astype(jnp.float32) + 1.0)
    cotangent = (out_grad.astype(jnp.float32) * loss_weight[:, :, None]).astype(jnp.bfloat16)
    cotangent = lax.optimization_barrier(cotangent)
    results = lax.map(one_document, (query, key_in, value_in, cotangent))
    norm_factor = 1.0 / math.sqrt(DOCS * L)
    bias_query = (lax.optimization_barrier(jnp.sum(results[1], axis=0)) * norm_factor).reshape(N_CTX, H * HD // N_CTX)
    bias_pair = jnp.stack([lax.optimization_barrier(jnp.sum(results[3], axis=0)), lax.optimization_barrier(jnp.sum(results[5], axis=0))]) * norm_factor
    return (results[0], results[2], results[4], bias_query, bias_pair)
```

```python
import math

import jax
import jax.numpy as jnp
from jax import lax
from jax.experimental import pallas as pl
from jax.experimental.pallas import tpu as pltpu
from jax.sharding import PartitionSpec as P

HD = 128
NB = 16
GROUP = 4
CHIPS = 8
CORES = 2
CTX = CHIPS * CORES
DP = 32
TOK = 64
DOCS = 2
SLOTS = 8
TILE = 4
QW = GROUP * HD
INV_ROOT = 1.0 / math.sqrt(HD)
EXP_SCALE = INV_ROOT * math.log2(math.e)

F32 = jnp.float32
BF16 = jnp.bfloat16


def nt(a, b):
    return lax.dot_general(a, b, (((1,), (1,)), ((), ())), preferred_element_type=F32)


def nn(a, b):
    return lax.dot_general(a, b, (((1,), (0,)), ((), ())), preferred_element_type=F32)


def kernel(
    q_hbm, k_hbm, v_hbm, o_hbm, masked, bucket,
    dq_out, dk_out, dv_out, bias_out,
    q_in, k_in, v_in, o_in, qc_stage, kv_stage, qc_buf, kv_buf, dq_stage, dkv_stage, dkv_buf,
    kt, dk_acc, dv_acc, bias_src, bias_all, msg, dp_buf,
    in_sem, qc_send, qc_recv, kv_send, kv_recv, dq_send, dq_recv, dkv_send, dkv_recv, bias_sem, dp_sem,
):
    me = lax.axis_index("ctx")
    dp = lax.axis_index("dp")
    y, c = lax.div(me, 2), lax.rem(me, 2)

    loads = [
        pltpu.make_async_copy(src, dst, in_sem.at[n])
        for n, (src, dst) in enumerate(((k_hbm, k_in), (v_hbm, v_in), (q_hbm, q_in), (o_hbm, o_in)))
    ]
    for load in loads:
        load.start()

    barrier = pltpu.get_barrier_semaphore()

    def greet_ctx(s, _):
        pl.semaphore_signal(barrier, inc=1, device_id={"ctx": lax.rem(me + s, CTX)})
        return 0

    def greet_dp(s, _):
        pl.semaphore_signal(barrier, inc=1, device_id={"dp": lax.rem(dp + s, DP)})
        return 0

    lax.fori_loop(1, CTX, greet_ctx, 0)
    lax.fori_loop(1, DP, greet_dp, 0)

    def remote(src, dst, send, recv, device):
        return pltpu.make_async_remote_copy(
            src_ref=src, dst_ref=dst, send_sem=send, recv_sem=recv, device_id=device
        )

    def far_first(n):
        half = lax.div(n + 1, 2)
        return 8 + half * (2 * lax.rem(n, 2) - 1)

    loads[0].wait()
    loads[1].wait()
    for d in range(DOCS):
        for g in range(CHIPS):
            kv_stage[d, g, :, 0:HD] = k_in[d, :, g * HD : (g + 1) * HD]
            kv_stage[d, g, :, HD : 2 * HD] = v_in[d, :, g * HD : (g + 1) * HD]

    pl.semaphore_wait(barrier, CTX - 1 + DP - 1)

    def send_kv(k):
        own = lax.rem(y, 4) + 4 * k
        pltpu.make_async_copy(kv_stage.at[c, own], kv_buf.at[k, me], kv_recv.at[k]).start()

        def one(n, _):
            j = lax.rem(me + far_first(n), CTX)
            d = lax.rem(j, 2)
            g = lax.rem(lax.div(j, 2), 4) + 4 * k
            remote(
                kv_stage.at[d, g], kv_buf.at[k, me], kv_send.at[k], kv_recv.at[k], {"ctx": j}
            ).start()
            return 0

        lax.fori_loop(0, CTX - 1, one, 0)

    def send_qc(k):
        own = lax.rem(y, 4) + 4 * k
        for a, step in ((3, 2 + 4 * c), (1, 1), (2, 7)):
            t = lax.rem(y + step, CHIPS)
            g = lax.rem(t, 4) + 4 * k
            for d in range(DOCS):
                remote(
                    qc_stage.at[d, g], qc_buf.at[k, 2 * a + c], qc_send.at[k], qc_recv.at[k],
                    {"ctx": 2 * t + d},
                ).start()
        remote(
            qc_stage.at[1 - c, own], qc_buf.at[k, c], qc_send.at[k], qc_recv.at[k],
            {"ctx": 2 * y + 1 - c},
        ).start()
        pltpu.make_async_copy(qc_stage.at[c, own], qc_buf.at[k, c], qc_recv.at[k]).start()

    send_kv(0)

    loads[2].wait()
    loads[3].wait()
    rows = lax.broadcasted_iota(jnp.int32, (TOK, 1), 0)
    diagonal = lax.broadcasted_iota(jnp.int32, (TOK, TOK), 0) == lax.broadcasted_iota(
        jnp.int32, (TOK, TOK), 1
    )
    for d in range(DOCS):
        hit = masked[d : d + 1, :] == rows + me * TOK
        is_masked = jnp.max(jnp.where(hit, 1.0, 0.0), axis=1, keepdims=True)
        row = bucket[d : d + 1, :].astype(F32)
        column = jnp.sum(jnp.where(diagonal, row, 0.0), axis=1, keepdims=True)
        weight = is_masked * NB / (column + 1.0)
        for g in range(CHIPS):
            qc_stage[d, g, :, 0:QW] = q_in[d, :, g * QW : (g + 1) * QW]
            grads = o_in[d, :, g * QW : (g + 1) * QW].astype(F32)
            qc_stage[d, g, :, QW : 2 * QW] = (grads * weight).astype(BF16)

    send_qc(0)
    send_kv(1)
    send_qc(1)

    def whole(ref, sem):
        pltpu.make_async_copy(ref, ref, sem).wait()

    bias_src[...] = jnp.zeros_like(bias_src)
    for k in range(2):
        own = lax.rem(y, 4) + 4 * k
        whole(kv_buf.at[k], kv_recv.at[k])
        whole(qc_buf.at[k], qc_recv.at[k])
        kt[...] = kv_buf[k, :, :, 0:HD].reshape(CTX * TOK, HD).T
        dk_acc[...] = jnp.zeros_like(dk_acc)
        dv_acc[...] = jnp.zeros_like(dv_acc)

        def step(n, _):
            h, part = lax.div(n, 2), lax.rem(n, 2)
            slots = pl.ds(part * TILE, TILE)
            q_cols = pl.ds(pl.multiple_of(h * HD, HD), HD)
            c_cols = pl.ds(pl.multiple_of(h * HD + QW, HD), HD)
            q = qc_buf[k, slots, :, q_cols].reshape(TILE * TOK, HD)
            cot = qc_buf[k, slots, :, c_cols].reshape(TILE * TOK, HD)
            keys = kv_buf[k, :, :, 0:HD].reshape(CTX * TOK, HD)
            values = kv_buf[k, :, :, HD : 2 * HD].reshape(CTX * TOK, HD)
            scores = nt(keys, q)
            top = jnp.max(scores, axis=0, keepdims=True)
            exponent = jnp.exp2((scores - top) * EXP_SCALE)
            probs = exponent * (1.0 / jnp.sum(exponent, axis=0, keepdims=True))
            probs_low = probs.astype(BF16)
            prob_grad = nt(values, cot)
            delta = jnp.sum(probs_low.astype(F32) * prob_grad, axis=0, keepdims=True)
            score_grad = (probs * (prob_grad - delta) * INV_ROOT).astype(BF16)
            dv_acc[...] += nn(probs_low, cot)
            dk_acc[...] += nn(score_grad, q)
            grad = nn(kt[...], score_grad).T
            dq_stage[k, slots, :, q_cols] = grad.astype(BF16).reshape(TILE, TOK, HD)
            bias_src[pl.ds(k * GROUP + h, 1), :] += jnp.sum(grad, axis=0, keepdims=True)
            return 0

        lax.fori_loop(0, GROUP * SLOTS // TILE, step, 0)
        bias_src[8 + k : 9 + k, :] = jnp.sum(dk_acc[...], axis=0, keepdims=True)
        bias_src[10 + k : 11 + k, :] = jnp.sum(dv_acc[...], axis=0, keepdims=True)
        dkv_stage[k, :, :, 0:HD] = dk_acc[...].astype(BF16).reshape(CTX, TOK, HD)
        dkv_stage[k, :, :, HD : 2 * HD] = dv_acc[...].astype(BF16).reshape(CTX, TOK, HD)

        if k == 1:
            pltpu.make_async_copy(bias_src, bias_all.at[me], bias_sem.at[1]).start()

            def send_bias(s, _):
                remote(
                    bias_src, bias_all.at[me], bias_sem.at[0], bias_sem.at[1],
                    {"ctx": lax.rem(me + s, CTX)},
                ).start()
                return 0

            lax.fori_loop(1, CTX, send_bias, 0)

        centre = lax.div(y, 4)

        def send_dkv(n, _):
            j = lax.rem(me + far_first(n), CTX)
            remote(
                dkv_stage.at[k, j], dkv_buf.at[centre, c, own], dkv_send.at[k], dkv_recv,
                {"ctx": j},
            ).start()
            return 0

        lax.fori_loop(0, CTX - 1, send_dkv, 0)
        pltpu.make_async_copy(
            dkv_stage.at[k, me], dkv_buf.at[centre, c, own], dkv_recv
        ).start()

        out_cols = pl.ds(pl.multiple_of(own * QW, QW), QW)
        for a, back in ((3, None), (1, 7), (2, 1)):
            for core in range(CORES):
                step_back = 6 - 4 * core if back is None else back
                j = 2 * lax.rem(y + step_back, CHIPS) + core
                remote(
                    dq_stage.at[k, 2 * a + core], dq_out.at[c, :, out_cols], dq_send.at[k],
                    dq_recv, {"ctx": j},
                ).start()
        remote(
            dq_stage.at[k, 1 - c], dq_out.at[c, :, out_cols], dq_send.at[k], dq_recv,
            {"ctx": 2 * y + 1 - c},
        ).start()
        pltpu.make_async_copy(dq_stage.at[k, c], dq_out.at[c, :, out_cols], dq_recv).start()

    whole(bias_all, bias_sem.at[1])
    first = lax.rem(y, 4) * 2
    q_row = lax.div(y, 4) * GROUP + 2 * c
    msg[...] = jnp.zeros_like(msg)
    for b in range(2):
        total = sum(bias_all[first + n, pl.ds(q_row + b, 1), :] for n in (0, 1, 8, 9))
        for a in range(4 * b, 4 * b + 4):
            msg[a, 0:1, :] = total
    for g in range(CHIPS):
        m, k = g % 4, g // 4
        for row, at in ((1, 8 + k), (2, 10 + k)):
            msg[g, row : row + 1, :] = sum(
                bias_all[2 * m + n, at : at + 1, :] for n in (0, 1, 8, 9)
            )
    pltpu.make_async_copy(msg.at[lax.div(dp, 4)], dp_buf.at[dp], dp_sem.at[1]).start()

    def send_msg(s, _):
        j = lax.rem(dp + s, DP)
        remote(
            msg.at[lax.div(j, 4)], dp_buf.at[dp], dp_sem.at[0], dp_sem.at[1], {"dp": j}
        ).start()
        return 0

    lax.fori_loop(1, DP, send_msg, 0)

    whole(dkv_buf, dkv_recv)
    for d in range(DOCS):
        for g in range(CHIPS):
            both = dkv_buf[0, d, g].astype(F32) + dkv_buf[1, d, g].astype(F32)
            dk_out[d, :, g * HD : (g + 1) * HD] = both[:, 0:HD].astype(BF16)
            dv_out[d, :, g * HD : (g + 1) * HD] = both[:, HD : 2 * HD].astype(BF16)

    whole(dp_buf, dp_sem.at[1])
    bias_out[...] = jnp.sum(dp_buf[...], axis=0) * (1.0 / 256.0)
    whole(dq_out, dq_recv)

    for k in range(2):
        whole(kv_buf.at[k, pl.ds(0, CTX - 1)], kv_send.at[k])
        whole(qc_buf.at[k, pl.ds(0, SLOTS - 1)], qc_send.at[k])
        whole(dkv_stage.at[k, pl.ds(0, CTX - 1)], dkv_send.at[k])
        whole(dq_stage.at[k, pl.ds(0, SLOTS - 1)], dq_send.at[k])
    whole(bias_all.at[pl.ds(0, CTX - 1)], bias_sem.at[0])
    whole(dp_buf.at[pl.ds(0, DP - 1)], dp_sem.at[0])


def per_device(query, key_in, value_in, out_grad, masked, bucket):
    vmem = pl.BlockSpec(memory_space=pltpu.VMEM)
    hbm = pl.BlockSpec(memory_space=pl.ANY)
    dma = pltpu.SemaphoreType.DMA
    query_grad, key_grad, value_grad, bias = pl.pallas_call(
        kernel,
        out_shape=(
            jax.ShapeDtypeStruct(query.shape, BF16),
            jax.ShapeDtypeStruct(key_in.shape, BF16),
            jax.ShapeDtypeStruct(value_in.shape, BF16),
            jax.ShapeDtypeStruct((8, HD), F32),
        ),
        in_specs=[hbm, hbm, hbm, hbm, vmem, vmem],
        out_specs=(hbm, vmem, vmem, vmem),
        scratch_shapes=[
            pltpu.VMEM(query.shape, BF16),
            pltpu.VMEM(key_in.shape, BF16),
            pltpu.VMEM(value_in.shape, BF16),
            pltpu.VMEM(out_grad.shape, BF16),
            pltpu.VMEM((DOCS, CHIPS, TOK, 2 * QW), BF16),
            pltpu.VMEM((DOCS, CHIPS, TOK, 2 * HD), BF16),
            pltpu.VMEM((2, SLOTS, TOK, 2 * QW), BF16),
            pltpu.VMEM((2, CTX, TOK, 2 * HD), BF16),
            pltpu.VMEM((2, SLOTS, TOK, QW), BF16),
            pltpu.VMEM((2, CTX, TOK, 2 * HD), BF16),
            pltpu.VMEM((2, DOCS, CHIPS, TOK, 2 * HD), BF16),
            pltpu.VMEM((HD, CTX * TOK), BF16),
            pltpu.VMEM((CTX * TOK, HD), F32),
            pltpu.VMEM((CTX * TOK, HD), F32),
            pltpu.VMEM((16, HD), F32),
            pltpu.VMEM((CTX, 16, HD), F32),
            pltpu.VMEM((CHIPS, 8, HD), F32),
            pltpu.VMEM((DP, 8, HD), F32),
            dma((4,)),
            dma((2,)),
            dma((2,)),
            dma((2,)),
            dma((2,)),
            dma((2,)),
            dma,
            dma((2,)),
            dma,
            dma((2,)),
            dma((2,)),
        ],
        compiler_params=pltpu.CompilerParams(
            collective_id=0, has_side_effects=True, vmem_limit_bytes=40 * 1024 * 1024
        ),
        cost_estimate=pl.CostEstimate(
            flops=6 * 10**9, bytes_accessed=8 * 10**6, transcendentals=4 * 10**6
        ),
    )(query, key_in, value_in, out_grad, masked, bucket)
    dp = lax.axis_index("dp")
    query_piece = lax.dynamic_slice(bias, (0, 8 * (dp % 16)), (1, 8))
    pair_piece = lax.dynamic_slice(bias, (1, 32 * (dp % 4)), (2, 32))
    return query_grad, key_grad, value_grad, query_piece, pair_piece


def solution(mesh):
    tokens = P("dp", "ctx", None)
    return jax.shard_map(
        per_device,
        mesh=mesh,
        in_specs=(tokens, tokens, tokens, tokens, P("dp", None), P("dp", "ctx")),
        out_specs=(tokens, tokens, tokens, P("ctx", "dp"), P(None, "dp")),
        check_vma=False,
    )
```

```python
import math

import jax
import jax.numpy as jnp
from jax import lax
from jax.experimental import pallas as pl
from jax.experimental.pallas import tpu as pltpu
from jax.sharding import PartitionSpec as P

HD = 128
NB = 16
GROUP = 4
CHIPS = 8
CORES = 2
CTX = CHIPS * CORES
DP = 32
TOK = 64
DOCS = 2
SLOTS = 8
TILE = 4
AHEAD = 5
QW = GROUP * HD
INV_ROOT = 1.0 / math.sqrt(HD)
EXP_SCALE = INV_ROOT * math.log2(math.e)

F32 = jnp.float32
BF16 = jnp.bfloat16


def nt(a, b):
    return lax.dot_general(a, b, (((1,), (1,)), ((), ())), preferred_element_type=F32)


def nn(a, b):
    return lax.dot_general(a, b, (((1,), (0,)), ((), ())), preferred_element_type=F32)


def kernel(
    q_hbm, k_hbm, v_hbm, o_hbm, masked_hbm, bucket_hbm,
    dq_out, dkv_out, bias_out,
    q_in, k_in, v_in, o_in, masked, bucket, qc_stage, kv_stage, qc_buf, kv_buf, dq_stage, dkv_stage,
    kt, dk_acc, dv_acc, bias_src, bias_all, msg, dp_buf, bias_sum, bias_in,
    in_sem, qc_send, qc_recv, kv_send, kv_recv, dq_send, dq_recv, dkv_send, dkv_recv,
    bias_send, bias_recv, dp_sem, share_sem, go_sem,
):
    me = lax.axis_index("ctx")
    dp = lax.axis_index("dp")
    y, c = lax.div(me, 2), lax.rem(me, 2)

    loads = [
        pltpu.make_async_copy(src, dst, in_sem.at[n])
        for n, (src, dst) in enumerate(
            (
                (k_hbm, k_in), (v_hbm, v_in), (q_hbm, q_in), (o_hbm, o_in),
                (masked_hbm, masked), (bucket_hbm, bucket),
            )
        )
    ]
    for load in loads:
        load.start()

    barrier = pltpu.get_barrier_semaphore()

    def greet_other(n, _):
        pl.semaphore_signal(barrier, inc=1, device_id={"ctx": 2 * lax.rem(y + n, CHIPS)})
        return 0

    def greet_dp(s, _):
        pl.semaphore_signal(barrier, inc=1, device_id={"dp": lax.rem(dp + s, DP)})
        return 0

    lax.fori_loop(1, CHIPS, greet_other, 0)

    @pl.when(c == 1)
    def _():
        pl.semaphore_signal(barrier, inc=1, device_id={"ctx": me - 1})
        lax.fori_loop(1, DP, greet_dp, 0)

    def remote(src, dst, send, recv, device):
        return pltpu.make_async_remote_copy(
            src_ref=src, dst_ref=dst, send_sem=send, recv_sem=recv, device_id=device
        )

    def far_first(n):
        half = lax.div(n + 1, 2)
        return 8 + half * (2 * lax.rem(n, 2) - 1)

    loads[0].wait()
    loads[1].wait()
    for d in range(DOCS):
        for g in range(CHIPS):
            kv_stage[d, g, :, 0:HD] = k_in[d, :, g * HD : (g + 1) * HD]
            kv_stage[d, g, :, HD : 2 * HD] = v_in[d, :, g * HD : (g + 1) * HD]

    @pl.when(c == 0)
    def _():
        pl.semaphore_wait(barrier, CTX - 1)
        pl.semaphore_signal(go_sem, inc=1, device_id={"ctx": me + 1})

    @pl.when(c == 1)
    def _():
        pl.semaphore_wait(go_sem, 1)

    def send_kv(k):
        own = lax.rem(y, 4) + 4 * k
        pltpu.make_async_copy(kv_stage.at[c, own], kv_buf.at[k, me], kv_recv.at[k]).start()

        def one(n, _):
            j = lax.rem(me + far_first(n), CTX)
            d = lax.rem(j, 2)
            g = lax.rem(lax.div(j, 2), 4) + 4 * k
            remote(
                kv_stage.at[d, g], kv_buf.at[k, me], kv_send.at[k], kv_recv.at[k], {"ctx": j}
            ).start()
            return 0

        lax.fori_loop(0, CTX - 1, one, 0)

    def send_qc(k):
        own = lax.rem(y, 4) + 4 * k
        for a, step in ((3, 2 + 4 * c), (1, 1), (2, 7)):
            t = lax.rem(y + step, CHIPS)
            g = lax.rem(t, 4) + 4 * k
            for d in range(DOCS):
                remote(
                    qc_stage.at[d, g], qc_buf.at[k, 2 * a + c], qc_send.at[k], qc_recv.at[k],
                    {"ctx": 2 * t + d},
                ).start()
        remote(
            qc_stage.at[1 - c, own], qc_buf.at[k, c], qc_send.at[k], qc_recv.at[k],
            {"ctx": 2 * y + 1 - c},
        ).start()
        pltpu.make_async_copy(qc_stage.at[c, own], qc_buf.at[k, c], qc_recv.at[k]).start()

    send_kv(0)

    for load in loads[2:]:
        load.wait()
    rows = lax.broadcasted_iota(jnp.int32, (TOK, 1), 0)
    diagonal = lax.broadcasted_iota(jnp.int32, (TOK, TOK), 0) == lax.broadcasted_iota(
        jnp.int32, (TOK, TOK), 1
    )
    for d in range(DOCS):
        hit = masked[d : d + 1, :] == rows + me * TOK
        is_masked = jnp.max(jnp.where(hit, 1.0, 0.0), axis=1, keepdims=True)
        row = bucket[d : d + 1, :].astype(F32)
        column = jnp.sum(jnp.where(diagonal, row, 0.0), axis=1, keepdims=True)
        weight = is_masked * NB / (column + 1.0)
        for g in range(CHIPS):
            qc_stage[d, g, :, 0:QW] = q_in[d, :, g * QW : (g + 1) * QW]
            grads = o_in[d, :, g * QW : (g + 1) * QW].astype(F32)
            qc_stage[d, g, :, QW : 2 * QW] = (grads * weight).astype(BF16)

    send_qc(0)
    send_kv(1)
    send_qc(1)

    def whole(ref, sem):
        pltpu.make_async_copy(ref, ref, sem).wait()

    def reduce_bias():
        for k in range(2):
            whole(bias_all.at[k], bias_recv.at[k])
        first = lax.rem(y, 4) * 2
        msg[...] = jnp.zeros_like(msg)
        for core in range(CORES):
            for b in range(2):
                row = 2 * core + b
                total = sum(
                    bias_all[lax.div(y, 4), first + n, row : row + 1, :] for n in (0, 1, 8, 9)
                )
                for a in range(4 * b, 4 * b + 4):
                    msg[a, core : core + 1, :] = total
        for g in range(CHIPS):
            m, k = g % 4, g // 4
            msg[g, 2:4, :] = sum(
                bias_all[k, 2 * m + n, GROUP : GROUP + 2, :] for n in (0, 1, 8, 9)
            )
        pl.semaphore_wait(barrier, DP - 1)
        pltpu.make_async_copy(msg.at[lax.div(dp, 4)], dp_buf.at[dp], dp_sem.at[1]).start()

        def send_msg(s, _):
            j = lax.rem(dp + s, DP)
            remote(
                msg.at[lax.div(j, 4)], dp_buf.at[dp], dp_sem.at[0], dp_sem.at[1], {"dp": j}
            ).start()
            return 0

        lax.fori_loop(1, DP, send_msg, 0)

    bias_src[...] = jnp.zeros_like(bias_src)
    for k in range(2):
        own = lax.rem(y, 4) + 4 * k
        whole(kv_buf.at[k], kv_recv.at[k])
        whole(qc_buf.at[k], qc_recv.at[k])
        kt[...] = kv_buf[k, :, :, 0:HD].reshape(CTX * TOK, HD).T
        dk_acc[...] = jnp.zeros_like(dk_acc)
        dv_acc[...] = jnp.zeros_like(dv_acc)

        def step(n, _):
            h, part = lax.div(n, 2), lax.rem(n, 2)
            slots = pl.ds(part * TILE, TILE)
            q_cols = pl.ds(pl.multiple_of(h * HD, HD), HD)
            c_cols = pl.ds(pl.multiple_of(h * HD + QW, HD), HD)
            q = qc_buf[k, slots, :, q_cols].reshape(TILE * TOK, HD)
            cot = qc_buf[k, slots, :, c_cols].reshape(TILE * TOK, HD)
            keys = kv_buf[k, :, :, 0:HD].reshape(CTX * TOK, HD)
            values = kv_buf[k, :, :, HD : 2 * HD].reshape(CTX * TOK, HD)
            scores = nt(keys, q)
            top = jnp.max(scores, axis=0, keepdims=True)
            exponent = jnp.exp2((scores - top) * EXP_SCALE)
            probs = exponent * (1.0 / jnp.sum(exponent, axis=0, keepdims=True))
            probs_low = probs.astype(BF16)
            prob_grad = nt(values, cot)
            delta = jnp.sum(probs_low.astype(F32) * prob_grad, axis=0, keepdims=True)
            score_grad = (probs * (prob_grad - delta) * INV_ROOT).astype(BF16)
            dv_acc[...] += nn(probs_low, cot)
            dk_acc[...] += nn(score_grad, q)
            grad = nn(kt[...], score_grad).T
            dq_stage[k, slots, :, q_cols] = grad.astype(BF16).reshape(TILE, TOK, HD)
            bias_src[k, pl.ds(h, 1), :] += jnp.sum(grad, axis=0, keepdims=True)
            return 0

        lax.fori_loop(0, GROUP * SLOTS // TILE, step, 0)
        bias_src[k, GROUP : GROUP + 1, :] = jnp.sum(dk_acc[...], axis=0, keepdims=True)
        bias_src[k, GROUP + 1 : GROUP + 2, :] = jnp.sum(dv_acc[...], axis=0, keepdims=True)
        dkv_stage[k, :, :, 0:HD] = dk_acc[...].astype(BF16).reshape(CTX, TOK, HD)
        dkv_stage[k, :, :, HD : 2 * HD] = dv_acc[...].astype(BF16).reshape(CTX, TOK, HD)

        def send_bias(n, _):
            remote(
                bias_src.at[k], bias_all.at[k, me], bias_send.at[k], bias_recv.at[k],
                {"ctx": 2 * lax.rem(y + n, CHIPS) + 1},
            ).start()
            return 0

        lax.fori_loop(1, CHIPS, send_bias, 0)

        @pl.when(c == 0)
        def _():
            remote(
                bias_src.at[k], bias_all.at[k, me], bias_send.at[k], bias_recv.at[k],
                {"ctx": me + 1},
            ).start()

        @pl.when(c == 1)
        def _():
            pltpu.make_async_copy(bias_src.at[k], bias_all.at[k, me], bias_recv.at[k]).start()

        out_cols = pl.ds(pl.multiple_of(own * QW, QW), QW)
        for a, back in ((3, None), (1, 7), (2, 1)):
            for core in range(CORES):
                step_back = 6 - 4 * core if back is None else back
                j = 2 * lax.rem(y + step_back, CHIPS) + core
                remote(
                    dq_stage.at[k, 2 * a + core], dq_out.at[c, :, out_cols], dq_send.at[k],
                    dq_recv, {"ctx": j},
                ).start()
        remote(
            dq_stage.at[k, 1 - c], dq_out.at[c, :, out_cols], dq_send.at[k], dq_recv,
            {"ctx": 2 * y + 1 - c},
        ).start()
        pltpu.make_async_copy(dq_stage.at[k, c], dq_out.at[c, :, out_cols], dq_recv).start()

        centre = lax.div(y, 4)

        def send_dkv(n, _):
            j = lax.rem(me + far_first(n), CTX)
            remote(
                dkv_stage.at[k, j], dkv_out.at[centre, c, own], dkv_send.at[k], dkv_recv,
                {"ctx": j},
            ).start()
            return 0

        ahead = 15 if k == 0 else AHEAD
        lax.fori_loop(0, ahead, send_dkv, 0)
        if k == 1:
            pl.when(c == 1)(reduce_bias)
        lax.fori_loop(ahead, CTX - 1, send_dkv, 0)
        pltpu.make_async_copy(
            dkv_stage.at[k, me], dkv_out.at[centre, c, own], dkv_recv
        ).start()

    whole(dkv_out, dkv_recv)
    whole(dq_out, dq_recv)
    @pl.when(c == 1)
    def _():
        whole(dp_buf, dp_sem.at[1])
        bias_sum[...] = jnp.sum(dp_buf[...], axis=0) * (1.0 / 256.0)
        share = remote(bias_sum, bias_in, share_sem.at[0], share_sem.at[1], {"ctx": me - 1})
        share.start()
        bias_out[...] = bias_sum[...]
        share.wait_send()
        whole(dp_buf.at[pl.ds(0, DP - 1)], dp_sem.at[0])

    @pl.when(c == 0)
    def _():
        whole(bias_in, share_sem.at[1])
        bias_out[...] = bias_in[...]


    for k in range(2):
        whole(kv_buf.at[k, pl.ds(0, CTX - 1)], kv_send.at[k])
        whole(qc_buf.at[k, pl.ds(0, SLOTS - 1)], qc_send.at[k])
        whole(dkv_stage.at[k, pl.ds(0, CTX - 1)], dkv_send.at[k])
        whole(dq_stage.at[k, pl.ds(0, SLOTS - 1)], dq_send.at[k])

    @pl.when(c == 0)
    def _():
        for k in range(2):
            whole(bias_all.at[k, pl.ds(0, CHIPS)], bias_send.at[k])

    @pl.when(c == 1)
    def _():
        for k in range(2):
            whole(bias_all.at[k, pl.ds(0, CHIPS - 1)], bias_send.at[k])


def finish(dq, dkv, bias, dq_out, dk_out, dv_out, q_out, kv_out, sem):
    copy = pltpu.make_async_copy(dq, dq_out, sem)
    copy.start()
    dp = lax.axis_index("dp")
    first = lax.rem(lax.axis_index("ctx"), 2) == 0
    q_rows = jnp.where(first, bias[0:1, :], bias[1:2, :])
    q_out[...] = pltpu.roll(q_rows, lax.rem(HD - 8 * lax.rem(dp, 16), HD), 1)[:, 0:8]
    kv_out[...] = pltpu.roll(bias[2:4, :], lax.rem(HD - 32 * lax.rem(dp, 4), HD), 1)[:, 0:32]
    for d in range(DOCS):
        for g in range(CHIPS):
            both = dkv[0, d, g].astype(F32) + dkv[1, d, g].astype(F32)
            dk_out[d, :, g * HD : (g + 1) * HD] = both[:, 0:HD].astype(BF16)
            dv_out[d, :, g * HD : (g + 1) * HD] = both[:, HD : 2 * HD].astype(BF16)
    copy.wait()


def per_device(query, key_in, value_in, out_grad, masked, bucket):
    vmem = pl.BlockSpec(memory_space=pltpu.VMEM)
    hbm = pl.BlockSpec(memory_space=pl.ANY)
    dma = pltpu.SemaphoreType.DMA
    args = (
        pltpu.with_memory_space_constraint(x, pltpu.HBM)
        for x in (query, key_in, value_in, out_grad, masked, bucket)
    )
    dq, dkv, bias = pl.pallas_call(
        kernel,
        out_shape=(
            jax.ShapeDtypeStruct(query.shape, BF16),
            jax.ShapeDtypeStruct((2, DOCS, CHIPS, TOK, 2 * HD), BF16),
            jax.ShapeDtypeStruct((8, HD), F32),
        ),
        in_specs=[hbm] * 6,
        out_specs=(hbm, hbm, vmem),
        scratch_shapes=[
            pltpu.VMEM(query.shape, BF16),
            pltpu.VMEM(key_in.shape, BF16),
            pltpu.VMEM(value_in.shape, BF16),
            pltpu.VMEM(out_grad.shape, BF16),
            pltpu.VMEM(masked.shape, jnp.int32),
            pltpu.VMEM(bucket.shape, jnp.int32),
            pltpu.VMEM((DOCS, CHIPS, TOK, 2 * QW), BF16),
            pltpu.VMEM((DOCS, CHIPS, TOK, 2 * HD), BF16),
            pltpu.VMEM((2, SLOTS, TOK, 2 * QW), BF16),
            pltpu.VMEM((2, CTX, TOK, 2 * HD), BF16),
            pltpu.VMEM((2, SLOTS, TOK, QW), BF16),
            pltpu.VMEM((2, CTX, TOK, 2 * HD), BF16),
            pltpu.VMEM((HD, CTX * TOK), BF16),
            pltpu.VMEM((CTX * TOK, HD), F32),
            pltpu.VMEM((CTX * TOK, HD), F32),
            pltpu.VMEM((2, 8, HD), F32),
            pltpu.VMEM((2, CTX, 8, HD), F32),
            pltpu.VMEM((CHIPS, 8, HD), F32),
            pltpu.VMEM((DP, 8, HD), F32),
            pltpu.VMEM((8, HD), F32),
            pltpu.VMEM((8, HD), F32),
            dma((6,)),
            dma((2,)),
            dma((2,)),
            dma((2,)),
            dma((2,)),
            dma((2,)),
            dma,
            dma((2,)),
            dma,
            dma((2,)),
            dma((2,)),
            dma((2,)),
            dma((2,)),
            pltpu.SemaphoreType.REGULAR,
        ],
        compiler_params=pltpu.CompilerParams(
            collective_id=0, has_side_effects=True, vmem_limit_bytes=40 * 1024 * 1024
        ),
        cost_estimate=pl.CostEstimate(
            flops=6 * 10**9, bytes_accessed=8 * 10**6, transcendentals=4 * 10**6
        ),
    )(*args)
    return pl.pallas_call(
        finish,
        out_shape=(
            jax.ShapeDtypeStruct(query.shape, BF16),
            jax.ShapeDtypeStruct(key_in.shape, BF16),
            jax.ShapeDtypeStruct(value_in.shape, BF16),
            jax.ShapeDtypeStruct((1, 8), F32),
            jax.ShapeDtypeStruct((2, 32), F32),
        ),
        in_specs=[hbm, vmem, vmem],
        out_specs=(hbm, vmem, vmem, vmem, vmem),
        scratch_shapes=[dma],
        compiler_params=pltpu.CompilerParams(vmem_limit_bytes=32 * 1024 * 1024),
    )(dq, dkv, bias)


def solution(mesh):
    tokens = P("dp", "ctx", None)
    return jax.shard_map(
        per_device,
        mesh=mesh,
        in_specs=(tokens, tokens, tokens, tokens, P("dp", None), P("dp", "ctx")),
        out_specs=(tokens, tokens, tokens, P("ctx", "dp"), P(None, "dp")),
        check_vma=False,
    )
```

```python
import math

import jax
import jax.numpy as jnp
from jax import lax
from jax.experimental import pallas as pl
from jax.experimental.pallas import tpu as pltpu
from jax.sharding import PartitionSpec as P

HD = 128
NB = 16
GROUP = 4
CHIPS = 8
CORES = 2
CTX = CHIPS * CORES
DP = 32
TOK = 64
DOCS = 2
SLOTS = 8
TILE = 8
AHEAD = 5
QW = GROUP * HD
INV_ROOT = 1.0 / math.sqrt(HD)
EXP_SCALE = INV_ROOT * math.log2(math.e)

F32 = jnp.float32
BF16 = jnp.bfloat16


def nt(a, b):
    return lax.dot_general(a, b, (((1,), (1,)), ((), ())), preferred_element_type=F32)


def nn(a, b):
    return lax.dot_general(a, b, (((1,), (0,)), ((), ())), preferred_element_type=F32)


def kernel(
    q_hbm, k_hbm, v_hbm, o_hbm, masked_hbm, bucket_hbm,
    dq_out, dkv_out, bias_out,
    q_in, k_in, v_in, o_in, masked, bucket, qc_stage, kv_stage, qc_buf, kv_buf, dq_stage, dkv_stage,
    kt, dk_acc, dv_acc, bias_src, bias_all, msg, dp_buf, bias_sum, bias_in,
    in_sem, qc_send, qc_recv, kv_send, kv_recv, dq_send, dq_recv, dkv_send, dkv_recv,
    bias_send, bias_recv, dp_sem, share_sem, go_sem,
):
    me = lax.axis_index("ctx")
    dp = lax.axis_index("dp")
    y, c = lax.div(me, 2), lax.rem(me, 2)

    loads = [
        pltpu.make_async_copy(src, dst, in_sem.at[n])
        for n, (src, dst) in enumerate(
            (
                (k_hbm, k_in), (v_hbm, v_in), (q_hbm, q_in), (o_hbm, o_in),
                (masked_hbm, masked), (bucket_hbm, bucket),
            )
        )
    ]
    for load in loads:
        load.start()

    barrier = pltpu.get_barrier_semaphore()

    def greet_other(n, _):
        pl.semaphore_signal(barrier, inc=1, device_id={"ctx": 2 * lax.rem(y + n, CHIPS)})
        return 0

    def greet_dp(s, _):
        pl.semaphore_signal(barrier, inc=1, device_id={"dp": lax.rem(dp + s, DP)})
        return 0

    lax.fori_loop(1, CHIPS, greet_other, 0)

    @pl.when(c == 1)
    def _():
        pl.semaphore_signal(barrier, inc=1, device_id={"ctx": me - 1})
        lax.fori_loop(1, DP, greet_dp, 0)

    def remote(src, dst, send, recv, device):
        return pltpu.make_async_remote_copy(
            src_ref=src, dst_ref=dst, send_sem=send, recv_sem=recv, device_id=device
        )

    def far_first(n):
        half = lax.div(n + 1, 2)
        return 8 + half * (2 * lax.rem(n, 2) - 1)

    loads[0].wait()
    loads[1].wait()
    for d in range(DOCS):
        for g in range(CHIPS):
            kv_stage[d, g, :, 0:HD] = k_in[d, :, g * HD : (g + 1) * HD]
            kv_stage[d, g, :, HD : 2 * HD] = v_in[d, :, g * HD : (g + 1) * HD]

    @pl.when(c == 0)
    def _():
        pl.semaphore_wait(barrier, CTX - 1)
        pl.semaphore_signal(go_sem, inc=1, device_id={"ctx": me + 1})

    @pl.when(c == 1)
    def _():
        pl.semaphore_wait(go_sem, 1)

    def send_kv(k):
        own = lax.rem(y, 4) + 4 * k
        pltpu.make_async_copy(kv_stage.at[c, own], kv_buf.at[k, me], kv_recv.at[k]).start()

        def one(n, _):
            j = lax.rem(me + far_first(n), CTX)
            d = lax.rem(j, 2)
            g = lax.rem(lax.div(j, 2), 4) + 4 * k
            remote(
                kv_stage.at[d, g], kv_buf.at[k, me], kv_send.at[k], kv_recv.at[k], {"ctx": j}
            ).start()
            return 0

        lax.fori_loop(0, CTX - 1, one, 0)

    def send_qc(k):
        own = lax.rem(y, 4) + 4 * k
        for a, step in ((3, 2 + 4 * c), (1, 1), (2, 7)):
            t = lax.rem(y + step, CHIPS)
            g = lax.rem(t, 4) + 4 * k
            for d in range(DOCS):
                remote(
                    qc_stage.at[d, g], qc_buf.at[k, 2 * a + c], qc_send.at[k], qc_recv.at[k],
                    {"ctx": 2 * t + d},
                ).start()
        remote(
            qc_stage.at[1 - c, own], qc_buf.at[k, c], qc_send.at[k], qc_recv.at[k],
            {"ctx": 2 * y + 1 - c},
        ).start()
        pltpu.make_async_copy(qc_stage.at[c, own], qc_buf.at[k, c], qc_recv.at[k]).start()

    send_kv(0)

    for load in loads[2:]:
        load.wait()
    rows = lax.broadcasted_iota(jnp.int32, (TOK, 1), 0)
    diagonal = lax.broadcasted_iota(jnp.int32, (TOK, TOK), 0) == lax.broadcasted_iota(
        jnp.int32, (TOK, TOK), 1
    )
    for d in range(DOCS):
        hit = masked[d : d + 1, :] == rows + me * TOK
        is_masked = jnp.max(jnp.where(hit, 1.0, 0.0), axis=1, keepdims=True)
        row = bucket[d : d + 1, :].astype(F32)
        column = jnp.sum(jnp.where(diagonal, row, 0.0), axis=1, keepdims=True)
        weight = is_masked * NB / (column + 1.0)
        for g in range(CHIPS):
            qc_stage[d, g, :, 0:QW] = q_in[d, :, g * QW : (g + 1) * QW]
            grads = o_in[d, :, g * QW : (g + 1) * QW].astype(F32)
            qc_stage[d, g, :, QW : 2 * QW] = (grads * weight).astype(BF16)

    send_qc(0)
    send_kv(1)
    send_qc(1)

    def whole(ref, sem):
        pltpu.make_async_copy(ref, ref, sem).wait()

    def reduce_bias():
        for k in range(2):
            whole(bias_all.at[k], bias_recv.at[k])
        first = lax.rem(y, 4) * 2
        msg[...] = jnp.zeros_like(msg)
        for core in range(CORES):
            for b in range(2):
                row = 2 * core + b
                total = sum(
                    bias_all[lax.div(y, 4), first + n, row : row + 1, :] for n in (0, 1, 8, 9)
                )
                for a in range(4 * b, 4 * b + 4):
                    msg[a, core : core + 1, :] = total
        for g in range(CHIPS):
            m, k = g % 4, g // 4
            msg[g, 2:4, :] = sum(
                bias_all[k, 2 * m + n, GROUP : GROUP + 2, :] for n in (0, 1, 8, 9)
            )
        pl.semaphore_wait(barrier, DP - 1)
        pltpu.make_async_copy(msg.at[lax.div(dp, 4)], dp_buf.at[dp], dp_sem.at[1]).start()

        def send_msg(s, _):
            j = lax.rem(dp + s, DP)
            remote(
                msg.at[lax.div(j, 4)], dp_buf.at[dp], dp_sem.at[0], dp_sem.at[1], {"dp": j}
            ).start()
            return 0

        lax.fori_loop(1, DP, send_msg, 0)

    bias_src[...] = jnp.zeros_like(bias_src)
    for k in range(2):
        own = lax.rem(y, 4) + 4 * k
        whole(kv_buf.at[k], kv_recv.at[k])
        whole(qc_buf.at[k], qc_recv.at[k])
        kt[...] = kv_buf[k, :, :, 0:HD].reshape(CTX * TOK, HD).T
        dk_acc[...] = jnp.zeros_like(dk_acc)
        dv_acc[...] = jnp.zeros_like(dv_acc)

        def step(n, _):
            h, part = lax.div(n, SLOTS // TILE), lax.rem(n, SLOTS // TILE)
            slots = pl.ds(part * TILE, TILE)
            q_cols = pl.ds(pl.multiple_of(h * HD, HD), HD)
            c_cols = pl.ds(pl.multiple_of(h * HD + QW, HD), HD)
            q = qc_buf[k, slots, :, q_cols].reshape(TILE * TOK, HD)
            cot = qc_buf[k, slots, :, c_cols].reshape(TILE * TOK, HD)
            keys = kv_buf[k, :, :, 0:HD].reshape(CTX * TOK, HD)
            values = kv_buf[k, :, :, HD : 2 * HD].reshape(CTX * TOK, HD)
            scores = nt(keys, q)
            top = jnp.max(scores, axis=0, keepdims=True)
            exponent = jnp.exp2((scores - top) * EXP_SCALE)
            probs = exponent * (1.0 / jnp.sum(exponent, axis=0, keepdims=True))
            probs_low = probs.astype(BF16)
            prob_grad = nt(values, cot)
            delta = jnp.sum(probs_low.astype(F32) * prob_grad, axis=0, keepdims=True)
            score_grad = (probs * (prob_grad - delta) * INV_ROOT).astype(BF16)
            dv_acc[...] += nn(probs_low, cot)
            dk_acc[...] += nn(score_grad, q)
            grad = nn(kt[...], score_grad).T
            dq_stage[k, slots, :, q_cols] = grad.astype(BF16).reshape(TILE, TOK, HD)
            bias_src[k, pl.ds(h, 1), :] += jnp.sum(grad, axis=0, keepdims=True)
            return 0

        lax.fori_loop(0, GROUP * SLOTS // TILE, step, 0)
        bias_src[k, GROUP : GROUP + 1, :] = jnp.sum(dk_acc[...], axis=0, keepdims=True)
        bias_src[k, GROUP + 1 : GROUP + 2, :] = jnp.sum(dv_acc[...], axis=0, keepdims=True)
        dkv_stage[k, :, :, 0:HD] = dk_acc[...].astype(BF16).reshape(CTX, TOK, HD)
        dkv_stage[k, :, :, HD : 2 * HD] = dv_acc[...].astype(BF16).reshape(CTX, TOK, HD)

        def send_bias(n, _):
            remote(
                bias_src.at[k], bias_all.at[k, me], bias_send.at[k], bias_recv.at[k],
                {"ctx": 2 * lax.rem(y + n, CHIPS) + 1},
            ).start()
            return 0

        lax.fori_loop(1, CHIPS, send_bias, 0)

        @pl.when(c == 0)
        def _():
            remote(
                bias_src.at[k], bias_all.at[k, me], bias_send.at[k], bias_recv.at[k],
                {"ctx": me + 1},
            ).start()

        @pl.when(c == 1)
        def _():
            pltpu.make_async_copy(bias_src.at[k], bias_all.at[k, me], bias_recv.at[k]).start()

        out_cols = pl.ds(pl.multiple_of(own * QW, QW), QW)
        for a, back in ((3, None), (1, 7), (2, 1)):
            for core in range(CORES):
                step_back = 6 - 4 * core if back is None else back
                j = 2 * lax.rem(y + step_back, CHIPS) + core
                remote(
                    dq_stage.at[k, 2 * a + core], dq_out.at[c, :, out_cols], dq_send.at[k],
                    dq_recv, {"ctx": j},
                ).start()
        remote(
            dq_stage.at[k, 1 - c], dq_out.at[c, :, out_cols], dq_send.at[k], dq_recv,
            {"ctx": 2 * y + 1 - c},
        ).start()
        pltpu.make_async_copy(dq_stage.at[k, c], dq_out.at[c, :, out_cols], dq_recv).start()

        centre = lax.div(y, 4)

        def send_dkv(n, _):
            j = lax.rem(me + far_first(n), CTX)
            remote(
                dkv_stage.at[k, j], dkv_out.at[centre, c, own], dkv_send.at[k], dkv_recv,
                {"ctx": j},
            ).start()
            return 0

        ahead = 15 if k == 0 else AHEAD
        lax.fori_loop(0, ahead, send_dkv, 0)
        if k == 1:
            pl.when(c == 1)(reduce_bias)
        lax.fori_loop(ahead, CTX - 1, send_dkv, 0)
        pltpu.make_async_copy(
            dkv_stage.at[k, me], dkv_out.at[centre, c, own], dkv_recv
        ).start()

    whole(dkv_out, dkv_recv)
    whole(dq_out, dq_recv)
    @pl.when(c == 1)
    def _():
        whole(dp_buf, dp_sem.at[1])
        bias_sum[...] = jnp.sum(dp_buf[...], axis=0) * (1.0 / 256.0)
        share = remote(bias_sum, bias_in, share_sem.at[0], share_sem.at[1], {"ctx": me - 1})
        share.start()
        bias_out[...] = bias_sum[...]
        share.wait_send()
        whole(dp_buf.at[pl.ds(0, DP - 1)], dp_sem.at[0])

    @pl.when(c == 0)
    def _():
        whole(bias_in, share_sem.at[1])
        bias_out[...] = bias_in[...]


    for k in range(2):
        whole(kv_buf.at[k, pl.ds(0, CTX - 1)], kv_send.at[k])
        whole(qc_buf.at[k, pl.ds(0, SLOTS - 1)], qc_send.at[k])
        whole(dkv_stage.at[k, pl.ds(0, CTX - 1)], dkv_send.at[k])
        whole(dq_stage.at[k, pl.ds(0, SLOTS - 1)], dq_send.at[k])

    @pl.when(c == 0)
    def _():
        for k in range(2):
            whole(bias_all.at[k, pl.ds(0, CHIPS)], bias_send.at[k])

    @pl.when(c == 1)
    def _():
        for k in range(2):
            whole(bias_all.at[k, pl.ds(0, CHIPS - 1)], bias_send.at[k])


def finish(dq, dkv, bias, dq_out, dk_out, dv_out, q_out, kv_out, sem):
    copy = pltpu.make_async_copy(dq, dq_out, sem)
    copy.start()
    dp = lax.axis_index("dp")
    first = lax.rem(lax.axis_index("ctx"), 2) == 0
    q_rows = jnp.where(first, bias[0:1, :], bias[1:2, :])
    q_out[...] = pltpu.roll(q_rows, lax.rem(HD - 8 * lax.rem(dp, 16), HD), 1)[:, 0:8]
    kv_out[...] = pltpu.roll(bias[2:4, :], lax.rem(HD - 32 * lax.rem(dp, 4), HD), 1)[:, 0:32]
    for d in range(DOCS):
        for g in range(CHIPS):
            both = dkv[0, d, g].astype(F32) + dkv[1, d, g].astype(F32)
            dk_out[d, :, g * HD : (g + 1) * HD] = both[:, 0:HD].astype(BF16)
            dv_out[d, :, g * HD : (g + 1) * HD] = both[:, HD : 2 * HD].astype(BF16)
    copy.wait()


def per_device(query, key_in, value_in, out_grad, masked, bucket):
    vmem = pl.BlockSpec(memory_space=pltpu.VMEM)
    hbm = pl.BlockSpec(memory_space=pl.ANY)
    dma = pltpu.SemaphoreType.DMA
    args = (
        pltpu.with_memory_space_constraint(x, pltpu.HBM)
        for x in (query, key_in, value_in, out_grad, masked, bucket)
    )
    dq, dkv, bias = pl.pallas_call(
        kernel,
        out_shape=(
            jax.ShapeDtypeStruct(query.shape, BF16),
            jax.ShapeDtypeStruct((2, DOCS, CHIPS, TOK, 2 * HD), BF16),
            jax.ShapeDtypeStruct((8, HD), F32),
        ),
        in_specs=[hbm] * 6,
        out_specs=(hbm, hbm, vmem),
        scratch_shapes=[
            pltpu.VMEM(query.shape, BF16),
            pltpu.VMEM(key_in.shape, BF16),
            pltpu.VMEM(value_in.shape, BF16),
            pltpu.VMEM(out_grad.shape, BF16),
            pltpu.VMEM(masked.shape, jnp.int32),
            pltpu.VMEM(bucket.shape, jnp.int32),
            pltpu.VMEM((DOCS, CHIPS, TOK, 2 * QW), BF16),
            pltpu.VMEM((DOCS, CHIPS, TOK, 2 * HD), BF16),
            pltpu.VMEM((2, SLOTS, TOK, 2 * QW), BF16),
            pltpu.VMEM((2, CTX, TOK, 2 * HD), BF16),
            pltpu.VMEM((2, SLOTS, TOK, QW), BF16),
            pltpu.VMEM((2, CTX, TOK, 2 * HD), BF16),
            pltpu.VMEM((HD, CTX * TOK), BF16),
            pltpu.VMEM((CTX * TOK, HD), F32),
            pltpu.VMEM((CTX * TOK, HD), F32),
            pltpu.VMEM((2, 8, HD), F32),
            pltpu.VMEM((2, CTX, 8, HD), F32),
            pltpu.VMEM((CHIPS, 8, HD), F32),
            pltpu.VMEM((DP, 8, HD), F32),
            pltpu.VMEM((8, HD), F32),
            pltpu.VMEM((8, HD), F32),
            dma((6,)),
            dma((2,)),
            dma((2,)),
            dma((2,)),
            dma((2,)),
            dma((2,)),
            dma,
            dma((2,)),
            dma,
            dma((2,)),
            dma((2,)),
            dma((2,)),
            dma((2,)),
            pltpu.SemaphoreType.REGULAR,
        ],
        compiler_params=pltpu.CompilerParams(
            collective_id=0, has_side_effects=True, vmem_limit_bytes=40 * 1024 * 1024
        ),
        cost_estimate=pl.CostEstimate(
            flops=6 * 10**9, bytes_accessed=8 * 10**6, transcendentals=4 * 10**6
        ),
    )(*args)
    return pl.pallas_call(
        finish,
        out_shape=(
            jax.ShapeDtypeStruct(query.shape, BF16),
            jax.ShapeDtypeStruct(key_in.shape, BF16),
            jax.ShapeDtypeStruct(value_in.shape, BF16),
            jax.ShapeDtypeStruct((1, 8), F32),
            jax.ShapeDtypeStruct((2, 32), F32),
        ),
        in_specs=[hbm, vmem, vmem],
        out_specs=(hbm, vmem, vmem, vmem, vmem),
        scratch_shapes=[dma],
        compiler_params=pltpu.CompilerParams(vmem_limit_bytes=32 * 1024 * 1024),
    )(dq, dkv, bias)


def solution(mesh):
    tokens = P("dp", "ctx", None)
    return jax.shard_map(
        per_device,
        mesh=mesh,
        in_specs=(tokens, tokens, tokens, tokens, P("dp", None), P("dp", "ctx")),
        out_specs=(tokens, tokens, tokens, P("ctx", "dp"), P(None, "dp")),
        check_vma=False,
    )
```

```python
import math

import jax
import jax.numpy as jnp
from jax import lax
from jax.experimental import pallas as pl
from jax.experimental.pallas import tpu as pltpu
from jax.sharding import PartitionSpec as P

HD = 128
NB = 16
GROUP = 4
CHIPS = 8
CORES = 2
CTX = CHIPS * CORES
DP = 32
TOK = 64
DOCS = 2
SLOTS = 8
TILE = 8
AHEAD = 5
QW = GROUP * HD
INV_ROOT = 1.0 / math.sqrt(HD)
EXP_SCALE = INV_ROOT * math.log2(math.e)

F32 = jnp.float32
BF16 = jnp.bfloat16


def nt(a, b):
    return lax.dot_general(a, b, (((1,), (1,)), ((), ())), preferred_element_type=F32)


def nn(a, b):
    return lax.dot_general(a, b, (((1,), (0,)), ((), ())), preferred_element_type=F32)


def kernel(
    q_hbm, k_hbm, v_hbm, o_hbm, masked_hbm, bucket_hbm,
    dq_out, dkv_out, bias_out,
    q_in, k_in, v_in, o_in, masked, bucket, qc_stage, kv_stage, qc_buf, kv_buf, dq_stage, dkv_stage,
    kt, dk_acc, dv_acc, bias_src, bias_all, q_src, q_all, msg, dp_buf, bias_sum, bias_in,
    in_sem, qc_send, qc_recv, kv_send, kv_recv, dq_send, dq_recv, dkv_send, dkv_recv,
    bias_send, bias_recv, q_send, q_recv, dp_sem, share_sem, go_sem,
):
    me = lax.axis_index("ctx")
    dp = lax.axis_index("dp")
    y, c = lax.div(me, 2), lax.rem(me, 2)

    loads = [
        pltpu.make_async_copy(src, dst, in_sem.at[n])
        for n, (src, dst) in enumerate(
            (
                (k_hbm, k_in), (v_hbm, v_in), (q_hbm, q_in), (o_hbm, o_in),
                (masked_hbm, masked), (bucket_hbm, bucket),
            )
        )
    ]
    for load in loads:
        load.start()

    barrier = pltpu.get_barrier_semaphore()

    def greet_other(n, _):
        pl.semaphore_signal(barrier, inc=1, device_id={"ctx": 2 * lax.rem(y + n, CHIPS)})
        return 0

    def greet_dp(s, _):
        pl.semaphore_signal(barrier, inc=1, device_id={"dp": lax.rem(dp + s, DP)})
        return 0

    lax.fori_loop(1, CHIPS, greet_other, 0)

    @pl.when(c == 1)
    def _():
        pl.semaphore_signal(barrier, inc=1, device_id={"ctx": me - 1})
        lax.fori_loop(1, DP, greet_dp, 0)

    def remote(src, dst, send, recv, device):
        return pltpu.make_async_remote_copy(
            src_ref=src, dst_ref=dst, send_sem=send, recv_sem=recv, device_id=device
        )

    def far_first(n):
        half = lax.div(n + 1, 2)
        return 8 + half * (2 * lax.rem(n, 2) - 1)

    loads[0].wait()
    loads[1].wait()
    for d in range(DOCS):
        for g in range(CHIPS):
            kv_stage[d, g, :, 0:HD] = k_in[d, :, g * HD : (g + 1) * HD]
            kv_stage[d, g, :, HD : 2 * HD] = v_in[d, :, g * HD : (g + 1) * HD]

    @pl.when(c == 0)
    def _():
        pl.semaphore_wait(barrier, CTX - 1)
        pl.semaphore_signal(go_sem, inc=1, device_id={"ctx": me + 1})

    @pl.when(c == 1)
    def _():
        pl.semaphore_wait(go_sem, 1)

    def send_kv(k):
        own = lax.rem(y, 4) + 4 * k
        pltpu.make_async_copy(kv_stage.at[c, own], kv_buf.at[k, me], kv_recv.at[k]).start()

        def one(n, _):
            j = lax.rem(me + far_first(n), CTX)
            d = lax.rem(j, 2)
            g = lax.rem(lax.div(j, 2), 4) + 4 * k
            remote(
                kv_stage.at[d, g], kv_buf.at[k, me], kv_send.at[k], kv_recv.at[k], {"ctx": j}
            ).start()
            return 0

        lax.fori_loop(0, CTX - 1, one, 0)

    def send_qc(k):
        own = lax.rem(y, 4) + 4 * k
        for a, step in ((3, 2 + 4 * c), (1, 1), (2, 7)):
            t = lax.rem(y + step, CHIPS)
            g = lax.rem(t, 4) + 4 * k
            for d in range(DOCS):
                remote(
                    qc_stage.at[d, g], qc_buf.at[k, 2 * a + c], qc_send.at[k], qc_recv.at[k],
                    {"ctx": 2 * t + d},
                ).start()
        remote(
            qc_stage.at[1 - c, own], qc_buf.at[k, c], qc_send.at[k], qc_recv.at[k],
            {"ctx": 2 * y + 1 - c},
        ).start()
        pltpu.make_async_copy(qc_stage.at[c, own], qc_buf.at[k, c], qc_recv.at[k]).start()

    send_kv(0)

    for load in loads[2:]:
        load.wait()
    rows = lax.broadcasted_iota(jnp.int32, (TOK, 1), 0)
    diagonal = lax.broadcasted_iota(jnp.int32, (TOK, TOK), 0) == lax.broadcasted_iota(
        jnp.int32, (TOK, TOK), 1
    )
    for d in range(DOCS):
        hit = masked[d : d + 1, :] == rows + me * TOK
        is_masked = jnp.max(jnp.where(hit, 1.0, 0.0), axis=1, keepdims=True)
        row = bucket[d : d + 1, :].astype(F32)
        column = jnp.sum(jnp.where(diagonal, row, 0.0), axis=1, keepdims=True)
        weight = is_masked * NB / (column + 1.0)
        for g in range(CHIPS):
            qc_stage[d, g, :, 0:QW] = q_in[d, :, g * QW : (g + 1) * QW]
            grads = o_in[d, :, g * QW : (g + 1) * QW].astype(F32)
            qc_stage[d, g, :, QW : 2 * QW] = (grads * weight).astype(BF16)

    send_qc(0)
    send_kv(1)
    send_qc(1)

    def whole(ref, sem):
        pltpu.make_async_copy(ref, ref, sem).wait()

    def reduce_bias():
        for k in range(2):
            whole(bias_all.at[k], bias_recv.at[k])
        whole(q_all, q_recv)
        msg[...] = jnp.zeros_like(msg)
        for core in range(CORES):
            for b in range(2):
                row = 2 * core + b
                total = sum(
                    q_all[n, row : row + 1, :] for n in range(4)
                )
                for a in range(4 * b, 4 * b + 4):
                    msg[a, core : core + 1, :] = total
        for g in range(CHIPS):
            m, k = g % 4, g // 4
            msg[g, 2:4, :] = sum(
                bias_all[k, 2 * m + n, :, :] for n in (0, 1, 8, 9)
            )
        pl.semaphore_wait(barrier, DP - 1)
        pltpu.make_async_copy(msg.at[lax.div(dp, 4)], dp_buf.at[dp], dp_sem.at[1]).start()

        def send_msg(s, _):
            j = lax.rem(dp + s, DP)
            remote(
                msg.at[lax.div(j, 4)], dp_buf.at[dp], dp_sem.at[0], dp_sem.at[1], {"dp": j}
            ).start()
            return 0

        lax.fori_loop(1, DP, send_msg, 0)

    for k in range(2):
        own = lax.rem(y, 4) + 4 * k
        whole(kv_buf.at[k], kv_recv.at[k])
        whole(qc_buf.at[k], qc_recv.at[k])
        kt[...] = kv_buf[k, :, :, 0:HD].reshape(CTX * TOK, HD).T
        dk_acc[...] = jnp.zeros_like(dk_acc)
        dv_acc[...] = jnp.zeros_like(dv_acc)

        def step(n, _):
            h, part = lax.div(n, SLOTS // TILE), lax.rem(n, SLOTS // TILE)
            slots = pl.ds(part * TILE, TILE)
            q_cols = pl.ds(pl.multiple_of(h * HD, HD), HD)
            c_cols = pl.ds(pl.multiple_of(h * HD + QW, HD), HD)
            q = qc_buf[k, slots, :, q_cols].reshape(TILE * TOK, HD)
            cot = qc_buf[k, slots, :, c_cols].reshape(TILE * TOK, HD)
            keys = kv_buf[k, :, :, 0:HD].reshape(CTX * TOK, HD)
            values = kv_buf[k, :, :, HD : 2 * HD].reshape(CTX * TOK, HD)
            scores = nt(keys, q)
            top = jnp.max(scores, axis=0, keepdims=True)
            exponent = jnp.exp2((scores - top) * EXP_SCALE)
            probs = exponent * (1.0 / jnp.sum(exponent, axis=0, keepdims=True))
            probs_low = probs.astype(BF16)
            prob_grad = nt(values, cot)
            delta = jnp.sum(probs_low.astype(F32) * prob_grad, axis=0, keepdims=True)
            score_grad = (probs * (prob_grad - delta) * INV_ROOT).astype(BF16)
            dv_acc[...] += nn(probs_low, cot)
            dk_acc[...] += nn(score_grad, q)
            grad = nn(kt[...], score_grad).T
            dq_stage[k, slots, :, q_cols] = grad.astype(BF16).reshape(TILE, TOK, HD)
            q_src[k, pl.ds(h, 1), :] = jnp.sum(grad, axis=0, keepdims=True)
            return 0

        lax.fori_loop(0, GROUP * SLOTS // TILE, step, 0)
        bias_src[k, 0:1, :] = jnp.sum(dk_acc[...], axis=0, keepdims=True)
        bias_src[k, 1:2, :] = jnp.sum(dv_acc[...], axis=0, keepdims=True)
        dkv_stage[k, :, :, 0:HD] = dk_acc[...].astype(BF16).reshape(CTX, TOK, HD)
        dkv_stage[k, :, :, HD : 2 * HD] = dv_acc[...].astype(BF16).reshape(CTX, TOK, HD)

        q_dst = q_all.at[2 * lax.div(y, 4) + c]
        stays = jnp.logical_and(c == 1, lax.div(y, 4) == k)

        @pl.when(stays)
        def _():
            pltpu.make_async_copy(q_src.at[k], q_dst, q_recv).start()

        @pl.when(jnp.logical_not(stays))
        def _():
            remote(q_src.at[k], q_dst, q_send.at[k], q_recv, {"ctx": 2 * own + 1}).start()

        def send_bias(n, _):
            remote(
                bias_src.at[k], bias_all.at[k, me], bias_send.at[k], bias_recv.at[k],
                {"ctx": 2 * lax.rem(y + n, CHIPS) + 1},
            ).start()
            return 0

        lax.fori_loop(1, CHIPS, send_bias, 0)

        @pl.when(c == 0)
        def _():
            remote(
                bias_src.at[k], bias_all.at[k, me], bias_send.at[k], bias_recv.at[k],
                {"ctx": me + 1},
            ).start()

        @pl.when(c == 1)
        def _():
            pltpu.make_async_copy(bias_src.at[k], bias_all.at[k, me], bias_recv.at[k]).start()

        out_cols = pl.ds(pl.multiple_of(own * QW, QW), QW)
        for a, back in ((3, None), (1, 7), (2, 1)):
            for core in range(CORES):
                step_back = 6 - 4 * core if back is None else back
                j = 2 * lax.rem(y + step_back, CHIPS) + core
                remote(
                    dq_stage.at[k, 2 * a + core], dq_out.at[c, :, out_cols], dq_send.at[k],
                    dq_recv, {"ctx": j},
                ).start()
        remote(
            dq_stage.at[k, 1 - c], dq_out.at[c, :, out_cols], dq_send.at[k], dq_recv,
            {"ctx": 2 * y + 1 - c},
        ).start()
        pltpu.make_async_copy(dq_stage.at[k, c], dq_out.at[c, :, out_cols], dq_recv).start()

        centre = lax.div(y, 4)

        def send_dkv(n, _):
            j = lax.rem(me + far_first(n), CTX)
            remote(
                dkv_stage.at[k, j], dkv_out.at[centre, c, own], dkv_send.at[k], dkv_recv,
                {"ctx": j},
            ).start()
            return 0

        ahead = 15 if k == 0 else AHEAD
        lax.fori_loop(0, ahead, send_dkv, 0)
        if k == 1:
            pl.when(c == 1)(reduce_bias)
        lax.fori_loop(ahead, CTX - 1, send_dkv, 0)
        pltpu.make_async_copy(
            dkv_stage.at[k, me], dkv_out.at[centre, c, own], dkv_recv
        ).start()

    whole(dkv_out, dkv_recv)
    whole(dq_out, dq_recv)
    @pl.when(c == 1)
    def _():
        whole(dp_buf, dp_sem.at[1])
        bias_sum[...] = jnp.sum(dp_buf[...], axis=0) * (1.0 / 256.0)
        share = remote(bias_sum, bias_in, share_sem.at[0], share_sem.at[1], {"ctx": me - 1})
        share.start()
        bias_out[...] = bias_sum[...]
        share.wait_send()
        whole(dp_buf.at[pl.ds(0, DP - 1)], dp_sem.at[0])

    @pl.when(c == 0)
    def _():
        whole(bias_in, share_sem.at[1])
        bias_out[...] = bias_in[...]


    for k in range(2):
        whole(kv_buf.at[k, pl.ds(0, CTX - 1)], kv_send.at[k])
        whole(qc_buf.at[k, pl.ds(0, SLOTS - 1)], qc_send.at[k])
        whole(dkv_stage.at[k, pl.ds(0, CTX - 1)], dkv_send.at[k])
        whole(dq_stage.at[k, pl.ds(0, SLOTS - 1)], dq_send.at[k])

    for k in range(2):

        @pl.when(jnp.logical_not(jnp.logical_and(c == 1, lax.div(y, 4) == k)))
        def _():
            whole(q_src.at[k], q_send.at[k])

    @pl.when(c == 0)
    def _():
        for k in range(2):
            whole(bias_all.at[k, pl.ds(0, CHIPS)], bias_send.at[k])

    @pl.when(c == 1)
    def _():
        for k in range(2):
            whole(bias_all.at[k, pl.ds(0, CHIPS - 1)], bias_send.at[k])


def finish(dq, dkv, bias, dq_out, dk_out, dv_out, q_out, kv_out, sem):
    copy = pltpu.make_async_copy(dq, dq_out, sem)
    copy.start()
    dp = lax.axis_index("dp")
    first = lax.rem(lax.axis_index("ctx"), 2) == 0
    q_rows = jnp.where(first, bias[0:1, :], bias[1:2, :])
    q_out[...] = pltpu.roll(q_rows, lax.rem(HD - 8 * lax.rem(dp, 16), HD), 1)[:, 0:8]
    kv_out[...] = pltpu.roll(bias[2:4, :], lax.rem(HD - 32 * lax.rem(dp, 4), HD), 1)[:, 0:32]
    for d in range(DOCS):
        for g in range(CHIPS):
            both = dkv[0, d, g].astype(F32) + dkv[1, d, g].astype(F32)
            dk_out[d, :, g * HD : (g + 1) * HD] = both[:, 0:HD].astype(BF16)
            dv_out[d, :, g * HD : (g + 1) * HD] = both[:, HD : 2 * HD].astype(BF16)
    copy.wait()


def per_device(query, key_in, value_in, out_grad, masked, bucket):
    vmem = pl.BlockSpec(memory_space=pltpu.VMEM)
    hbm = pl.BlockSpec(memory_space=pl.ANY)
    dma = pltpu.SemaphoreType.DMA
    args = (
        pltpu.with_memory_space_constraint(x, pltpu.HBM)
        for x in (query, key_in, value_in, out_grad, masked, bucket)
    )
    dq, dkv, bias = pl.pallas_call(
        kernel,
        out_shape=(
            jax.ShapeDtypeStruct(query.shape, BF16),
            jax.ShapeDtypeStruct((2, DOCS, CHIPS, TOK, 2 * HD), BF16),
            jax.ShapeDtypeStruct((8, HD), F32),
        ),
        in_specs=[hbm] * 6,
        out_specs=(hbm, hbm, vmem),
        scratch_shapes=[
            pltpu.VMEM(query.shape, BF16),
            pltpu.VMEM(key_in.shape, BF16),
            pltpu.VMEM(value_in.shape, BF16),
            pltpu.VMEM(out_grad.shape, BF16),
            pltpu.VMEM(masked.shape, jnp.int32),
            pltpu.VMEM(bucket.shape, jnp.int32),
            pltpu.VMEM((DOCS, CHIPS, TOK, 2 * QW), BF16),
            pltpu.VMEM((DOCS, CHIPS, TOK, 2 * HD), BF16),
            pltpu.VMEM((2, SLOTS, TOK, 2 * QW), BF16),
            pltpu.VMEM((2, CTX, TOK, 2 * HD), BF16),
            pltpu.VMEM((2, SLOTS, TOK, QW), BF16),
            pltpu.VMEM((2, CTX, TOK, 2 * HD), BF16),
            pltpu.VMEM((HD, CTX * TOK), BF16),
            pltpu.VMEM((CTX * TOK, HD), F32),
            pltpu.VMEM((CTX * TOK, HD), F32),
            pltpu.VMEM((2, 2, HD), F32),
            pltpu.VMEM((2, CTX, 2, HD), F32),
            pltpu.VMEM((2, GROUP, HD), F32),
            pltpu.VMEM((4, GROUP, HD), F32),
            pltpu.VMEM((CHIPS, 8, HD), F32),
            pltpu.VMEM((DP, 8, HD), F32),
            pltpu.VMEM((8, HD), F32),
            pltpu.VMEM((8, HD), F32),
            dma((6,)),
            dma((2,)),
            dma((2,)),
            dma((2,)),
            dma((2,)),
            dma((2,)),
            dma,
            dma((2,)),
            dma,
            dma((2,)),
            dma((2,)),
            dma((2,)),
            dma,
            dma((2,)),
            dma((2,)),
            pltpu.SemaphoreType.REGULAR,
        ],
        compiler_params=pltpu.CompilerParams(
            collective_id=0, has_side_effects=True, vmem_limit_bytes=40 * 1024 * 1024
        ),
        cost_estimate=pl.CostEstimate(
            flops=6 * 10**9, bytes_accessed=8 * 10**6, transcendentals=4 * 10**6
        ),
    )(*args)
    return pl.pallas_call(
        finish,
        out_shape=(
            jax.ShapeDtypeStruct(query.shape, BF16),
            jax.ShapeDtypeStruct(key_in.shape, BF16),
            jax.ShapeDtypeStruct(value_in.shape, BF16),
            jax.ShapeDtypeStruct((1, 8), F32),
            jax.ShapeDtypeStruct((2, 32), F32),
        ),
        in_specs=[hbm, vmem, vmem],
        out_specs=(hbm, vmem, vmem, vmem, vmem),
        scratch_shapes=[dma],
        compiler_params=pltpu.CompilerParams(vmem_limit_bytes=32 * 1024 * 1024),
    )(dq, dkv, bias)


def solution(mesh):
    tokens = P("dp", "ctx", None)
    return jax.shard_map(
        per_device,
        mesh=mesh,
        in_specs=(tokens, tokens, tokens, tokens, P("dp", None), P("dp", "ctx")),
        out_specs=(tokens, tokens, tokens, P("ctx", "dp"), P(None, "dp")),
        check_vma=False,
    )
```
